32 devices in a mesh: tm: 4 (over y, x), grid: 8 (over z, core).
Axes of the slice: x: 2, y: 2, z: 4, core: 2. Of those that a mesh axis runs over, the one named last changes fastest.
Arguments:
- clocked_seawarmth: bfloat16 [4096, 24576], P(('tm', 'grid')), may hold values from -12 to 12
- clocked_precipitation: bfloat16 [4096, 24576], P(('tm', 'grid')), may hold values from -12 to 12
- fading_weights: float32 [2, 4096], P(None, 'tm'), may hold values from 0.4 to 1, as said below
- starting_average: float32 [2, 24576], P(None, 'grid'), may hold values from -6 to 6
- warmth_random_operator: bfloat16 [24576, 256], P('grid'), may hold values from -0.0390625 to 0.0390625
- wetness_random_operator: bfloat16 [24576, 256], P('grid'), may hold values from -0.0390625 to 0.0390625
Outputs:
- warmth_summary: float32 [256, 24576], P('tm', 'grid')
- wetness_summary: float32 [256, 24576], P('tm', 'grid')
- kernel_middle: float32 [256, 256], replicated
The draws below stay inside these ranges and needn't reach their ends.
Inputs may be any that keep to these rules, and one draw needn't show every extreme that they name: `fading_weights`: each factor lies below one.
All inputs are finite; a program needn't handle non-finite values.
Results may differ from the reference program's by a relative error of at most 0.0085.
Values may be sent and summed in bfloat16 or wider, within the bound.
A program may use at most 192 MiB of HBM per device.

```python
import jax
import jax.numpy as jnp
from jax import lax

PROBE_COUNT = 256
SPAN_CLOCKTIMES = 4096
MESH_SITES = 24576


def draw_field(key):
    key_scale, key_values = jax.random.split(key, 2)
    point_scale = jnp.exp(jax.random.uniform(key_scale, (1, MESH_SITES), jnp.float32, jnp.log(0.3), jnp.log(3.0)))
    quantity_lines = jnp.clip(jax.random.normal(key_values, (SPAN_CLOCKTIMES, MESH_SITES), jnp.float32), -4.0, 4.0)
    return jnp.clip(quantity_lines * point_scale, -12.0, 12.0)


def draw_clocked_seawarmth(key, part):
    return draw_field(jax.random.fold_in(key, 101)).astype(jnp.bfloat16)


def draw_clocked_precipitation(key, part):
    return draw_field(jax.random.fold_in(key, 202)).astype(jnp.bfloat16)


def draw_fading_weights(key, part):
    divide_seeds = jax.random.split(jax.random.fold_in(key, 303), 6)
    slow_rate = jnp.exp(jax.random.uniform(divide_seeds[0], (2,), jnp.float32, jnp.log(0.0001), jnp.log(0.0003)))
    fast_rate = jnp.exp(jax.random.uniform(divide_seeds[1], (2,), jnp.float32, jnp.log(0.02), jnp.log(0.035)))
    chosen = jax.random.randint(divide_seeds[2], (), 0, 2)
    base_rate = jnp.where(jnp.arange(2) == chosen, fast_rate, slow_rate)
    roughness = jnp.exp(jax.random.uniform(divide_seeds[3], (2, SPAN_CLOCKTIMES), jnp.float32, jnp.log(0.5), jnp.log(2.0)))
    fading_multiplier = 1.0 - base_rate[:, None] * roughness
    spike_location = jax.random.randint(divide_seeds[4], (3,), 0, SPAN_CLOCKTIMES)
    spike_segment = jnp.any(jnp.arange(SPAN_CLOCKTIMES)[None, :] == spike_location[:, None], axis=0)
    spike_cutoff = jax.random.uniform(divide_seeds[5], (2, SPAN_CLOCKTIMES), jnp.float32, 0.5, 0.8)
    return jnp.where(spike_segment[None, :], fading_multiplier * spike_cutoff, fading_multiplier)


def block_levels(stream_key, shape, cuts, low, high):
    def one(dim, shards_of):
        heights = jax.random.uniform(jax.random.fold_in(jax.random.fold_in(stream_key, 6), dim), (shards_of,), jnp.float32, low / len(cuts), high / len(cuts))
        return jnp.repeat(jnp.exp(heights), shape[dim] // shards_of).reshape((-1,) + (1,) * (len(shape) - dim - 1))

    level = one(*cuts[0])
    for cut in cuts[1:]:
        level = level * one(*cut)
    return level


def noise(key, shape, spread, bound, cuts=(), held_as=jnp.bfloat16):
    array = spread * jax.random.normal(key, shape, jnp.float32)
    if cuts:
        array = array * block_levels(key, shape, cuts, -0.22, 0.18)
    return jnp.clip(array, -bound, bound).astype(held_as)


def setup_inputs(seed: int = 0) -> dict:
    arg_keys = jax.random.split(jax.random.key(seed), 7)
    return {
        "clocked_seawarmth": draw_clocked_seawarmth(jax.random.fold_in(arg_keys[6], 71), 0),
        "clocked_precipitation": draw_clocked_precipitation(jax.random.fold_in(arg_keys[6], 71), 0),
        "fading_weights": draw_fading_weights(jax.random.fold_in(arg_keys[6], 71), 0),
        "starting_average": noise(arg_keys[3], (2, MESH_SITES), 1.0, 6.0, ((1, 8),), jnp.float32),
        "warmth_random_operator": noise(arg_keys[4], (MESH_SITES, PROBE_COUNT), MESH_SITES ** -0.5, 0.0390625, ((0, 8),)),
        "wetness_random_operator": noise(arg_keys[5], (MESH_SITES, PROBE_COUNT), MESH_SITES ** -0.5, 0.0390625, ((0, 8),)),
    }


def reference(clocked_seawarmth, clocked_precipitation, fading_weights, starting_average, warmth_random_operator, wetness_random_operator):
    def march_once(running, single_tick_feed):
        warmth_line, wetness_line, fading_multiplier = single_tick_feed
        quantity_lines = jnp.stack([warmth_line, wetness_line]).astype(jnp.float32)
        departure_amount = (quantity_lines - running).astype(jnp.bfloat16)
        running = fading_multiplier[:, None] * running + (1.0 - fading_multiplier[:, None]) * quantity_lines
        return running, (departure_amount[0], departure_amount[1])

    final_running_average, departure_lines = lax.scan(march_once, starting_average.astype(jnp.float32), (clocked_seawarmth, clocked_precipitation, jnp.transpose(fading_weights)))
    warmth_departure, wetness_departure = departure_lines
    warmth_compressed = jnp.dot(warmth_departure, warmth_random_operator, preferred_element_type=jnp.float32).astype(jnp.bfloat16)
    wetness_compressed = jnp.dot(wetness_departure, wetness_random_operator, preferred_element_type=jnp.float32).astype(jnp.bfloat16)
    divisor_magnitude = SPAN_CLOCKTIMES ** -0.5
    warmth_summary = jnp.dot(jnp.transpose(wetness_compressed), warmth_departure, preferred_element_type=jnp.float32) * divisor_magnitude
    wetness_summary = jnp.dot(jnp.transpose(warmth_compressed), wetness_departure, preferred_element_type=jnp.float32) * divisor_magnitude
    kernel_middle = jnp.dot(jnp.transpose(warmth_compressed), wetness_compressed, preferred_element_type=jnp.float32) * divisor_magnitude
    return warmth_summary, wetness_summary, kernel_middle
```

```python
import functools

import jax
import jax.numpy as jnp
from jax import lax
from jax.experimental import pallas as pl
from jax.experimental.pallas import tpu as pltpu
from jax.sharding import Mesh, PartitionSpec as P

MESH = pl.DeviceIdType.MESH
VMEM_LIMIT = 56 * 1024 * 1024


def flip(index, mask, count):
    out, bit = 0, 1
    while bit < count:
        out = out + lax.rem(lax.div(index, bit) + (mask // bit) % 2, 2) * bit
        bit *= 2
    return out


def greet(count, where):
    barrier = pltpu.get_barrier_semaphore()
    for mask in range(1, count):
        pl.semaphore_signal(barrier, inc=1, device_id=where(mask), device_id_type=MESH)
    pl.semaphore_wait(barrier, count - 1)


def group_peer(mask, nb):
    mine = lax.axis_index("tm") * 2 + lax.axis_index("cc")
    peer = flip(mine, mask, nb)
    return peer, (lax.div(peer, 2), lax.axis_index("zz"), lax.rem(peer, 2))


def exchange_kernel(nt, nz, sub, warm, wet, out, send_sem, recv_sem, own_sem):
    nb = nt * 2
    mine = lax.axis_index("tm") * 2 + lax.axis_index("cc")
    greet(nb, lambda mask: group_peer(mask, nb)[1])

    def columns(block, z):
        start = (z * 2 + lax.rem(block, 2)) * (nt * sub) + lax.div(block, 2) * sub
        return pl.ds(pl.multiple_of(start, 128), sub)

    order = list(range(nb - 1, 0, -1))
    for f, source in enumerate((warm, wet)):
        for z in range(nz):
            for mask in order:
                peer, device = group_peer(mask, nb)
                pltpu.make_async_remote_copy(
                    src_ref=source.at[:, columns(peer, z)],
                    dst_ref=out.at[f, mine, :, pl.ds(z * sub, sub)],
                    send_sem=send_sem.at[f, mask - 1],
                    recv_sem=recv_sem.at[f, mask - 1],
                    device_id=device,
                    device_id_type=MESH,
                ).start()
            pltpu.make_async_copy(
                source.at[:, columns(mine, z)],
                out.at[f, mine, :, pl.ds(z * sub, sub)],
                own_sem.at[f],
            ).start()
    for f in range(2):
        pltpu.make_async_copy(out.at[f, mine], out.at[f, mine], own_sem.at[f]).wait()
        for mask in order:
            peer, device = group_peer(mask, nb)
            whole = pltpu.make_async_remote_copy(
                src_ref=out.at[f, peer],
                dst_ref=out.at[f, peer],
                send_sem=send_sem.at[f, mask - 1],
                recv_sem=recv_sem.at[f, mask - 1],
                device_id=device,
                device_id_type=MESH,
            )
            whole.wait_send()
            whole.wait_recv()


def exchange(warm, wet, nt, nz, sub):
    nb = nt * 2
    hours = warm.shape[0]
    return pl.pallas_call(
        functools.partial(exchange_kernel, nt, nz, sub),
        out_shape=jax.ShapeDtypeStruct((2, nb, hours, nz * sub), jnp.bfloat16),
        in_specs=[pl.BlockSpec(memory_space=pl.ANY)] * 2,
        out_specs=pl.BlockSpec(memory_space=pl.ANY),
        scratch_shapes=[
            pltpu.SemaphoreType.DMA((2, nb - 1)),
            pltpu.SemaphoreType.DMA((2, nb - 1)),
            pltpu.SemaphoreType.DMA((2,)),
        ],
        compiler_params=pltpu.CompilerParams(collective_id=0, has_side_effects=True),
        cost_estimate=pl.CostEstimate(flops=10**11, bytes_accessed=10**8, transcendentals=0),
        name="exchange",
    )(warm, wet)


def ends_kernel(weights, x, ends):
    for f in range(2):
        for b in range(x.shape[1]):
            rows = jnp.dot(weights[f, b], x[f, b], preferred_element_type=jnp.float32)
            ends[f, b : b + 1, :] = jnp.sum(rows, axis=0, keepdims=True)


def block_ends(weights, x, sub):
    _, nb, hours, width = x.shape
    return pl.pallas_call(
        ends_kernel,
        grid=(width // sub,),
        out_shape=jax.ShapeDtypeStruct((2, nb, width), jnp.float32),
        in_specs=[
            pl.BlockSpec(weights.shape, lambda i: (0, 0, 0, 0)),
            pl.BlockSpec((2, nb, hours, sub), lambda i: (0, 0, 0, i)),
        ],
        out_specs=pl.BlockSpec((2, nb, sub), lambda i: (0, 0, i)),
        compiler_params=pltpu.CompilerParams(vmem_limit_bytes=VMEM_LIMIT),
        name="block_ends",
    )(weights, x)


def anomaly_kernel(nt, nz, gains, within, fade, ends, start, x, operator, anomaly, proj):
    nb = nt * 2
    z_mine = lax.axis_index("zz")

    @pl.when(pl.program_id(0) == 0)
    def _():
        proj[...] = jnp.zeros_like(proj)

    for f in range(2):
        level = start[0, f : f + 1, :]
        entering = [level] * nb
        for t in range(nt):
            for z in range(nz):
                for c in range(2):
                    b = t * 2 + c
                    entering[b] = jnp.where(z_mine == z, level, entering[b])
                    step = (t * nz + z) * 2 + c
                    level = gains[f, step] * level + ends[z, f, b : b + 1, :]
        for b in range(nb):
            values = x[f, b]
            twice = jnp.concatenate([values, values], axis=0)
            inside = jnp.dot(within[f, b], twice, preferred_element_type=jnp.float32)
            previous = inside + fade[f, b] * entering[b]
            departure = (values.astype(jnp.float32) - previous).astype(jnp.bfloat16)
            anomaly[f, b] = departure
            proj[f, b] += jnp.dot(departure, operator[f], preferred_element_type=jnp.float32)


def anomalies(gains, within, fade, ends, start, x, operator, nt, nz, sub):
    _, nb, hours, width = x.shape
    rank = operator.shape[-1]
    return pl.pallas_call(
        functools.partial(anomaly_kernel, nt, nz),
        grid=(nz,),
        out_shape=(
            jax.ShapeDtypeStruct(x.shape, jnp.bfloat16),
            jax.ShapeDtypeStruct((2, nb, hours, rank), jnp.float32),
        ),
        in_specs=[
            pl.BlockSpec(memory_space=pltpu.SMEM),
            pl.BlockSpec(within.shape, lambda i: (0, 0, 0, 0)),
            pl.BlockSpec(fade.shape, lambda i: (0, 0, 0, 0)),
            pl.BlockSpec((nz, 2, nb, sub), lambda i: (0, 0, 0, i)),
            pl.BlockSpec((1, 2, sub), lambda i: (i, 0, 0)),
            pl.BlockSpec((2, nb, hours, sub), lambda i: (0, 0, 0, i)),
            pl.BlockSpec((2, sub, rank), lambda i: (0, i, 0)),
        ],
        out_specs=(
            pl.BlockSpec((2, nb, hours, sub), lambda i: (0, 0, 0, i)),
            pl.BlockSpec((2, nb, hours, rank), lambda i: (0, 0, 0, 0)),
        ),
        compiler_params=pltpu.CompilerParams(vmem_limit_bytes=VMEM_LIMIT),
        name="anomalies",
    )(gains, within, fade, ends, start, x, operator)


def split(weights, count):
    parts = []
    for _ in range(count):
        part = weights.astype(jnp.bfloat16)
        parts.append(part)
        weights = weights - part.astype(jnp.float32)
    return parts


def over_hours(left, right):
    return lax.dot_general(
        left, right, (((0,), (0,)), ((), ())), preferred_element_type=jnp.float32
    )


def per_device(warm, wet, fading, starting, warmth_operator, wetness_operator):
    nt, nz = lax.axis_size("tm"), lax.axis_size("zz")
    t_mine, z_mine = lax.axis_index("tm"), lax.axis_index("zz")
    nb = nt * 2
    hours = warm.shape[0]
    sub = warm.shape[1] // (nb * nz)
    rank = warmth_operator.shape[1]

    operator = lax.dynamic_slice_in_dim(
        jnp.stack([warmth_operator, wetness_operator]), t_mine * sub, sub, axis=1
    )
    operator = lax.all_gather(operator, "zz", axis=1, tiled=True)
    start = lax.all_gather(lax.dynamic_slice_in_dim(starting, t_mine * sub, sub, axis=1), "zz")
    fading = lax.all_gather(fading, "tm", axis=1, tiled=True)

    x = exchange(warm, wet, nt, nz, sub)

    every = fading.reshape(2, nt, nz, 2, hours)
    gains = jnp.exp(jnp.sum(jnp.log(every), axis=-1)).reshape(2, nt * nz * 2)
    decay = lax.dynamic_index_in_dim(every, z_mine, 2, keepdims=False).reshape(2, nb, hours)
    log_decay = jnp.log(decay)
    row = lax.broadcasted_iota(jnp.int32, (hours, hours), 0)
    col = lax.broadcasted_iota(jnp.int32, (hours, hours), 1)
    inclusive = jnp.sum(jnp.where(row >= col, log_decay[:, :, None, :], 0.0), axis=-1)
    exclusive = inclusive - log_decay
    spread = exclusive[..., :, None] - inclusive[..., None, :]
    within = (
        jnp.where(row > col, jnp.exp(jnp.minimum(spread, 0.0)), 0.0)
        * (1.0 - decay)[..., None, :]
    )
    within = jnp.concatenate(split(within, 2), axis=-1)
    to_end = jnp.exp(inclusive[..., -1:] - inclusive) * (1.0 - decay)
    to_end = jnp.stack(split(to_end, 3), axis=2)
    to_end = jnp.pad(to_end, ((0, 0), (0, 0), (0, 13), (0, 0)))
    fade = jnp.exp(exclusive)[..., None]

    ends = lax.all_gather(block_ends(to_end, x, sub), "zz")
    anomaly, proj = anomalies(gains, within, fade, ends, start, x, operator, nt, nz, sub)
    share = lax.psum_scatter(
        proj.reshape(2, nb * hours, rank), ("tm", "cc"), scatter_dimension=1, tiled=True
    ).astype(jnp.bfloat16)
    lines = lax.all_gather(share, ("tm", "cc"), axis=1, tiled=True)
    anomaly = anomaly.reshape(2, nb * hours, nz * sub)
    scale = (nb * nz * hours) ** (-0.5)
    sketches = jnp.stack(
        [over_hours(lines[1], anomaly[0]), over_hours(lines[0], anomaly[1])]
    ).astype(jnp.bfloat16)
    middle = lax.psum(over_hours(lines[0], lines[1]), "zz") * scale
    sums = lax.psum_scatter(sketches, "zz", scatter_dimension=2, tiled=True)
    sums = lax.all_to_all(sums, "tm", split_axis=1, concat_axis=2, tiled=True)
    sums = sums.astype(jnp.float32) * scale
    return sums[0], sums[1], middle


def solution(mesh):
    nt, ng = mesh.devices.shape
    mesh = Mesh(mesh.devices.reshape(nt, ng // 2, 2), ("tm", "zz", "cc"))
    grid = ("zz", "cc")
    return jax.shard_map(
        per_device,
        mesh=mesh,
        in_specs=(
            P(("tm", "zz", "cc"), None),
            P(("tm", "zz", "cc"), None),
            P(None, "tm"),
            P(None, grid),
            P(grid, None),
            P(grid, None),
        ),
        out_specs=(P("tm", grid), P("tm", grid), P()),
        check_vma=False,
    )
```

```python
import functools

import jax
import jax.numpy as jnp
from jax import lax
from jax.experimental import pallas as pl
from jax.experimental.pallas import tpu as pltpu
from jax.sharding import Mesh, PartitionSpec as P

MESH = pl.DeviceIdType.MESH
VMEM_LIMIT = 56 * 1024 * 1024


def flip(index, mask, count):
    out, bit = 0, 1
    while bit < count:
        out = out + lax.rem(lax.div(index, bit) + (mask // bit) % 2, 2) * bit
        bit *= 2
    return out


def greet(count, where):
    barrier = pltpu.get_barrier_semaphore()
    for mask in range(1, count):
        pl.semaphore_signal(barrier, inc=1, device_id=where(mask), device_id_type=MESH)
    pl.semaphore_wait(barrier, count - 1)


def group_peer(mask, nb):
    mine = lax.axis_index("tm") * 2 + lax.axis_index("cc")
    peer = flip(mine, mask, nb)
    return peer, (lax.div(peer, 2), lax.axis_index("zz"), lax.rem(peer, 2))


def exchange_kernel(
    nt, nz, sub, warm, wet, fading, out, decays, send_sem, recv_sem, own_sem, fade_send, fade_recv
):
    nb = nt * 2
    mine = lax.axis_index("tm") * 2 + lax.axis_index("cc")
    greet(nb, lambda mask: group_peer(mask, nb)[1])

    def columns(block, z):
        start = (z * 2 + lax.rem(block, 2)) * (nt * sub) + lax.div(block, 2) * sub
        return pl.ds(pl.multiple_of(start, 128), sub)

    order = list(range(nb - 1, 0, -1))

    def fade_copy(mask):
        return pltpu.make_async_remote_copy(
            src_ref=fading,
            dst_ref=decays.at[mine],
            send_sem=fade_send.at[mask - 1],
            recv_sem=fade_recv.at[mask - 1],
            device_id=group_peer(mask, nb)[1],
            device_id_type=MESH,
        )

    for mask in order:
        fade_copy(mask).start()
    own_fade = pltpu.make_async_copy(fading, decays.at[mine], own_sem.at[2])
    own_fade.start()
    for f, source in enumerate((warm, wet)):
        for z in range(nz):
            for mask in order:
                peer, device = group_peer(mask, nb)
                pltpu.make_async_remote_copy(
                    src_ref=source.at[:, columns(peer, z)],
                    dst_ref=out.at[f, mine, :, pl.ds(z * sub, sub)],
                    send_sem=send_sem.at[f, mask - 1],
                    recv_sem=recv_sem.at[f, mask - 1],
                    device_id=device,
                    device_id_type=MESH,
                ).start()
            pltpu.make_async_copy(
                source.at[:, columns(mine, z)],
                out.at[f, mine, :, pl.ds(z * sub, sub)],
                own_sem.at[f],
            ).start()
    for f in range(2):
        pltpu.make_async_copy(out.at[f, mine], out.at[f, mine], own_sem.at[f]).wait()
        for mask in order:
            peer, device = group_peer(mask, nb)
            whole = pltpu.make_async_remote_copy(
                src_ref=out.at[f, peer],
                dst_ref=out.at[f, peer],
                send_sem=send_sem.at[f, mask - 1],
                recv_sem=recv_sem.at[f, mask - 1],
                device_id=device,
                device_id_type=MESH,
            )
            whole.wait_send()
            whole.wait_recv()
    own_fade.wait()
    for mask in order:
        fade_copy(mask).wait()


def exchange(warm, wet, fading, nt, nz, sub):
    nb = nt * 2
    hours = warm.shape[0]
    return pl.pallas_call(
        functools.partial(exchange_kernel, nt, nz, sub),
        out_shape=(
            jax.ShapeDtypeStruct((2, nb, hours, nz * sub), jnp.bfloat16),
            jax.ShapeDtypeStruct((nb,) + fading.shape, jnp.float32),
        ),
        in_specs=[pl.BlockSpec(memory_space=pl.ANY)] * 3,
        out_specs=(pl.BlockSpec(memory_space=pl.ANY),) * 2,
        scratch_shapes=[
            pltpu.SemaphoreType.DMA((2, nb - 1)),
            pltpu.SemaphoreType.DMA((2, nb - 1)),
            pltpu.SemaphoreType.DMA((3,)),
            pltpu.SemaphoreType.DMA((nb - 1,)),
            pltpu.SemaphoreType.DMA((nb - 1,)),
        ],
        compiler_params=pltpu.CompilerParams(collective_id=0, has_side_effects=True),
        cost_estimate=pl.CostEstimate(flops=10**11, bytes_accessed=10**8, transcendentals=0),
        name="exchange",
    )(warm, wet, fading)


def ends_kernel(weights, x, ends):
    for f in range(2):
        for b in range(x.shape[1]):
            rows = jnp.dot(weights[f, b], x[f, b], preferred_element_type=jnp.float32)
            ends[f, b : b + 1, :] = jnp.sum(rows, axis=0, keepdims=True)


def block_ends(weights, x, sub):
    _, nb, hours, width = x.shape
    return pl.pallas_call(
        ends_kernel,
        grid=(width // sub,),
        out_shape=jax.ShapeDtypeStruct((2, nb, width), jnp.float32),
        in_specs=[
            pl.BlockSpec(weights.shape, lambda i: (0, 0, 0, 0)),
            pl.BlockSpec((2, nb, hours, sub), lambda i: (0, 0, 0, i)),
        ],
        out_specs=pl.BlockSpec((2, nb, sub), lambda i: (0, 0, i)),
        compiler_params=pltpu.CompilerParams(vmem_limit_bytes=VMEM_LIMIT),
        name="block_ends",
    )(weights, x)


def anomaly_kernel(nt, nz, gains, within, fade, ends, start, x, operator, anomaly, proj, total):
    nb = nt * 2
    z_mine = lax.axis_index("zz")

    @pl.when(pl.program_id(0) == 0)
    def _():
        total[...] = jnp.zeros_like(total)

    for f in range(2):
        level = start[0, f : f + 1, :]
        entering = [level] * nb
        for t in range(nt):
            for z in range(nz):
                for c in range(2):
                    b = t * 2 + c
                    entering[b] = jnp.where(z_mine == z, level, entering[b])
                    step = (t * nz + z) * 2 + c
                    level = gains[f, step] * level + ends[z, f, b : b + 1, :]
        for b in range(nb):
            values = x[f, b]
            twice = jnp.concatenate([values, values], axis=0)
            inside = jnp.dot(within[f, b], twice, preferred_element_type=jnp.float32)
            previous = inside + fade[f, b] * entering[b]
            departure = (values.astype(jnp.float32) - previous).astype(jnp.bfloat16)
            anomaly[f, b] = departure
            total[b, f] += jnp.dot(departure, operator[0, f], preferred_element_type=jnp.float32)

    @pl.when(pl.program_id(0) == pl.num_programs(0) - 1)
    def _():
        proj[...] = total[...].astype(proj.dtype)


def anomalies(gains, within, fade, ends, start, x, operator, nt, nz, sub):
    _, nb, hours, width = x.shape
    rank = operator.shape[-1]
    return pl.pallas_call(
        functools.partial(anomaly_kernel, nt, nz),
        grid=(nz,),
        out_shape=(
            jax.ShapeDtypeStruct(x.shape, jnp.bfloat16),
            jax.ShapeDtypeStruct((nb, 2, hours, rank), jnp.bfloat16),
        ),
        in_specs=[
            pl.BlockSpec(memory_space=pltpu.SMEM),
            pl.BlockSpec(within.shape, lambda i: (0, 0, 0, 0)),
            pl.BlockSpec(fade.shape, lambda i: (0, 0, 0, 0)),
            pl.BlockSpec((nz, 2, nb, sub), lambda i: (0, 0, 0, i)),
            pl.BlockSpec((1, 2, sub), lambda i: (i, 0, 0)),
            pl.BlockSpec((2, nb, hours, sub), lambda i: (0, 0, 0, i)),
            pl.BlockSpec((1, 2, sub, rank), lambda i: (i, 0, 0, 0)),
        ],
        out_specs=(
            pl.BlockSpec((2, nb, hours, sub), lambda i: (0, 0, 0, i)),
            pl.BlockSpec((nb, 2, hours, rank), lambda i: (0, 0, 0, 0)),
        ),
        scratch_shapes=[pltpu.VMEM((nb, 2, hours, rank), jnp.float32)],
        compiler_params=pltpu.CompilerParams(vmem_limit_bytes=VMEM_LIMIT),
        name="anomalies",
    )(gains, within, fade, ends, start, x, operator)


def over_hours(left, right):
    return lax.dot_general(
        left, right, (((0,), (0,)), ((), ())), preferred_element_type=jnp.float32
    )


def sketch_kernel(
    nt, nz, sub, proj, anomaly, sketch, middle,
    held, parts, lines, cross, planes, rows,
    load_sem, part_send, part_recv, line_send, line_recv,
    plane_send, plane_recv, row_send, row_recv,
):
    nb = nt * 2
    t, z, c = lax.axis_index("tm"), lax.axis_index("zz"), lax.axis_index("cc")
    mine = t * 2 + c
    hours, rank = proj.shape[2:]
    share = rank // nb
    masks = range(1, nb)
    load = pltpu.make_async_copy(anomaly, held, load_sem)
    load.start()

    def z_peer(step):
        return (t, lax.rem(z + step, nz), c)

    barrier = pltpu.get_barrier_semaphore()
    for mask in masks:
        pl.semaphore_signal(barrier, inc=1, device_id=group_peer(mask, nb)[1], device_id_type=MESH)
    for step in range(1, nz):
        pl.semaphore_signal(barrier, inc=1, device_id=z_peer(step), device_id_type=MESH)
    pl.semaphore_wait(barrier, nb - 1 + nz - 1)

    def to_group(mask, src, dst, send, recv):
        return pltpu.make_async_remote_copy(
            src_ref=src,
            dst_ref=dst,
            send_sem=send.at[mask - 1],
            recv_sem=recv.at[mask - 1],
            device_id=group_peer(mask, nb)[1],
            device_id_type=MESH,
        )

    copies = [
        to_group(m, proj.at[group_peer(m, nb)[0]], parts.at[m - 1], part_send, part_recv)
        for m in masks
    ]
    for copy in copies:
        copy.start()
    total = proj[mine].astype(jnp.float32)
    for m, copy in zip(masks, copies):
        copy.wait_recv()
        total = total + parts[m - 1].astype(jnp.float32)
    lines[mine] = total.astype(jnp.bfloat16)
    for copy in copies:
        copy.wait_send()
    copies = [
        to_group(m, lines.at[mine], lines.at[mine], line_send, line_recv) for m in masks
    ]
    for copy in copies:
        copy.start()
    load.wait()
    for copy in copies:
        copy.wait()

    left = lines[:, 0].reshape(nb * hours, rank)
    right = lines[:, 1].reshape(nb * hours, rank)
    cross[...] = over_hours(left, right).reshape(nb, share, rank)
    copies = [
        pltpu.make_async_remote_copy(
            src_ref=cross.at[mine],
            dst_ref=planes.at[step - 1],
            send_sem=plane_send.at[step - 1],
            recv_sem=plane_recv.at[step - 1],
            device_id=z_peer(step),
            device_id_type=MESH,
        )
        for step in range(1, nz)
    ]
    for copy in copies:
        copy.start()

    def columns(i, f):
        cut = pl.ds(pl.multiple_of(i * sub, 128), sub)
        values = held[f, :, :, cut].reshape(nb * hours, sub)
        weights = lines[:, 1 - f].reshape(nb * hours, rank)
        sketch[f, :, cut] = over_hours(weights, values).astype(jnp.bfloat16)

    @pl.loop(0, nz)
    def _(i):
        columns(i, 0)

    for copy in copies:
        copy.wait()
    ordered = [cross[mine]] + [planes[step - 1] for step in range(1, nz)]
    summed = jnp.zeros_like(ordered[0])
    for plane in range(nz):
        for step in range(nz):
            summed = summed + jnp.where(lax.rem(z - step + nz, nz) == plane, ordered[step], 0.0)
    rows[mine] = summed
    copies = [to_group(m, rows.at[mine], rows.at[mine], row_send, row_recv) for m in masks]
    for copy in copies:
        copy.start()

    @pl.loop(0, nz)
    def _(i):
        columns(i, 1)

    for copy in copies:
        copy.wait()
    middle[...] = rows[...].reshape(rank, rank)


def sketches_of(proj, anomaly, nt, nz, sub):
    nb, _, hours, rank = proj.shape
    dma = pltpu.SemaphoreType.DMA
    return pl.pallas_call(
        functools.partial(sketch_kernel, nt, nz, sub),
        out_shape=(
            jax.ShapeDtypeStruct((2, rank, nz * sub), jnp.bfloat16),
            jax.ShapeDtypeStruct((rank, rank), jnp.float32),
        ),
        in_specs=[pl.BlockSpec(memory_space=pltpu.VMEM), pl.BlockSpec(memory_space=pl.ANY)],
        out_specs=(pl.BlockSpec(memory_space=pltpu.VMEM),) * 2,
        scratch_shapes=[
            pltpu.VMEM(anomaly.shape, jnp.bfloat16),
            pltpu.VMEM((nb - 1, 2, hours, rank), jnp.bfloat16),
            pltpu.VMEM((nb, 2, hours, rank), jnp.bfloat16),
            pltpu.VMEM((nb, rank // nb, rank), jnp.float32),
            pltpu.VMEM((nz - 1, rank // nb, rank), jnp.float32),
            pltpu.VMEM((nb, rank // nb, rank), jnp.float32),
            dma,
            dma((nb - 1,)),
            dma((nb - 1,)),
            dma((nb - 1,)),
            dma((nb - 1,)),
            dma((nz - 1,)),
            dma((nz - 1,)),
            dma((nb - 1,)),
            dma((nb - 1,)),
        ],
        compiler_params=pltpu.CompilerParams(
            collective_id=1, has_side_effects=True, vmem_limit_bytes=VMEM_LIMIT
        ),
        name="sketches",
    )(proj, anomaly)


def split(weights, count):
    parts = []
    for _ in range(count):
        part = lax.reduce_precision(weights, 8, 7)
        parts.append(part.astype(jnp.bfloat16))
        weights = weights - part
    return parts


def per_device(warm, wet, fading, starting, warmth_operator, wetness_operator):
    nt, nz = lax.axis_size("tm"), lax.axis_size("zz")
    t_mine, z_mine = lax.axis_index("tm"), lax.axis_index("zz")
    nb = nt * 2
    hours = warm.shape[0]
    sub = warm.shape[1] // (nb * nz)
    rank = warmth_operator.shape[1]

    tile = jnp.stack([warmth_operator, wetness_operator])
    average = jnp.stack(split(lax.dynamic_slice_in_dim(starting, t_mine * sub, sub, axis=1), 3), 1)
    average = average.reshape(2, -1, rank)
    extra = average.shape[1]
    average = jnp.pad(average, ((0, 0), (0, -extra % 16), (0, 0)))
    tile = lax.dynamic_slice_in_dim(tile, t_mine * sub, sub, axis=1)
    tiles = lax.all_gather(jnp.concatenate([tile, average], axis=1), "zz")
    terms = tiles[:, :, sub : sub + extra].reshape(nz, 2, 3, sub).astype(jnp.float32)
    start = terms[:, :, 0] + terms[:, :, 1] + terms[:, :, 2]

    x, decays = exchange(warm, wet, fading, nt, nz, sub)
    fading = jnp.concatenate([decays[2 * t] for t in range(nt)], axis=1)

    every = fading.reshape(2, nt, nz, 2, hours)
    gains = jnp.exp(jnp.sum(jnp.log(every), axis=-1)).reshape(2, nt * nz * 2)
    decay = lax.dynamic_index_in_dim(every, z_mine, 2, keepdims=False).reshape(2, nb, hours)
    log_decay = jnp.log(decay)
    row = lax.broadcasted_iota(jnp.int32, (hours, hours), 0)
    col = lax.broadcasted_iota(jnp.int32, (hours, hours), 1)
    inclusive = jnp.sum(jnp.where(row >= col, log_decay[:, :, None, :], 0.0), axis=-1)
    exclusive = inclusive - log_decay
    spread = exclusive[..., :, None] - inclusive[..., None, :]
    within = (
        jnp.where(row > col, jnp.exp(jnp.minimum(spread, 0.0)), 0.0)
        * (1.0 - decay)[..., None, :]
    )
    within = jnp.concatenate(split(within, 2), axis=-1)
    to_end = jnp.exp(inclusive[..., -1:] - inclusive) * (1.0 - decay)
    to_end = jnp.stack(split(to_end, 3), axis=2)
    to_end = jnp.pad(to_end, ((0, 0), (0, 0), (0, 13), (0, 0)))
    fade = jnp.exp(exclusive)[..., None]

    ends = lax.all_gather(block_ends(to_end, x, sub), "zz")
    anomaly, proj = anomalies(gains, within, fade, ends, start, x, tiles, nt, nz, sub)
    sketches, middle = sketches_of(proj, anomaly, nt, nz, sub)
    scale = (nb * nz * hours) ** (-0.5)
    sums = lax.psum_scatter(sketches, "zz", scatter_dimension=2, tiled=True)
    sums = lax.all_to_all(sums, "tm", split_axis=1, concat_axis=2, tiled=True)
    sums = sums.astype(jnp.float32) * scale
    return sums[0], sums[1], middle * scale


def solution(mesh):
    nt, ng = mesh.devices.shape
    mesh = Mesh(mesh.devices.reshape(nt, ng // 2, 2), ("tm", "zz", "cc"))
    grid = ("zz", "cc")
    return jax.shard_map(
        per_device,
        mesh=mesh,
        in_specs=(
            P(("tm", "zz", "cc"), None),
            P(("tm", "zz", "cc"), None),
            P(None, "tm"),
            P(None, grid),
            P(grid, None),
            P(grid, None),
        ),
        out_specs=(P("tm", grid), P("tm", grid), P()),
        check_vma=False,
    )
```

```python
import functools

import jax
import jax.numpy as jnp
from jax import lax
from jax.experimental import pallas as pl
from jax.experimental.pallas import tpu as pltpu
from jax.sharding import Mesh, PartitionSpec as P

MESH = pl.DeviceIdType.MESH
VMEM_LIMIT = 56 * 1024 * 1024


def flip(index, mask, count):
    out, bit = 0, 1
    while bit < count:
        out = out + lax.rem(lax.div(index, bit) + (mask // bit) % 2, 2) * bit
        bit *= 2
    return out


def greet(count, where):
    barrier = pltpu.get_barrier_semaphore()
    for mask in range(1, count):
        pl.semaphore_signal(barrier, inc=1, device_id=where(mask), device_id_type=MESH)
    pl.semaphore_wait(barrier, count - 1)


def group_peer(mask, nb):
    mine = lax.axis_index("tm") * 2 + lax.axis_index("cc")
    peer = flip(mine, mask, nb)
    return peer, (lax.div(peer, 2), lax.axis_index("zz"), lax.rem(peer, 2))


def exchange_kernel(
    nt, nz, sub, warm, wet, fading, out, decays, send_sem, recv_sem, own_sem, fade_send, fade_recv
):
    nb = nt * 2
    mine = lax.axis_index("tm") * 2 + lax.axis_index("cc")
    greet(nb, lambda mask: group_peer(mask, nb)[1])

    def columns(block, z):
        start = (z * 2 + lax.rem(block, 2)) * (nt * sub) + lax.div(block, 2) * sub
        return pl.ds(pl.multiple_of(start, 128), sub)

    order = list(range(nb - 1, 0, -1))

    def fade_copy(mask):
        return pltpu.make_async_remote_copy(
            src_ref=fading,
            dst_ref=decays.at[mine],
            send_sem=fade_send.at[mask - 1],
            recv_sem=fade_recv.at[mask - 1],
            device_id=group_peer(mask, nb)[1],
            device_id_type=MESH,
        )

    for mask in order:
        fade_copy(mask).start()
    own_fade = pltpu.make_async_copy(fading, decays.at[mine], own_sem.at[2])
    own_fade.start()
    for f, source in enumerate((warm, wet)):
        for z in range(nz):
            for mask in order:
                peer, device = group_peer(mask, nb)
                pltpu.make_async_remote_copy(
                    src_ref=source.at[:, columns(peer, z)],
                    dst_ref=out.at[f, mine, :, pl.ds(z * sub, sub)],
                    send_sem=send_sem.at[f, mask - 1],
                    recv_sem=recv_sem.at[f, mask - 1],
                    device_id=device,
                    device_id_type=MESH,
                ).start()
            pltpu.make_async_copy(
                source.at[:, columns(mine, z)],
                out.at[f, mine, :, pl.ds(z * sub, sub)],
                own_sem.at[f],
            ).start()
    for f in range(2):
        pltpu.make_async_copy(out.at[f, mine], out.at[f, mine], own_sem.at[f]).wait()
        for mask in order:
            peer, device = group_peer(mask, nb)
            whole = pltpu.make_async_remote_copy(
                src_ref=out.at[f, peer],
                dst_ref=out.at[f, peer],
                send_sem=send_sem.at[f, mask - 1],
                recv_sem=recv_sem.at[f, mask - 1],
                device_id=device,
                device_id_type=MESH,
            )
            whole.wait_send()
            whole.wait_recv()
    own_fade.wait()
    for mask in order:
        fade_copy(mask).wait()


def exchange(warm, wet, fading, nt, nz, sub):
    nb = nt * 2
    hours = warm.shape[0]
    return pl.pallas_call(
        functools.partial(exchange_kernel, nt, nz, sub),
        out_shape=(
            jax.ShapeDtypeStruct((2, nb, hours, nz * sub), jnp.bfloat16),
            jax.ShapeDtypeStruct((nb,) + fading.shape, jnp.float32),
        ),
        in_specs=[pl.BlockSpec(memory_space=pl.ANY)] * 3,
        out_specs=(pl.BlockSpec(memory_space=pl.ANY),) * 2,
        scratch_shapes=[
            pltpu.SemaphoreType.DMA((2, nb - 1)),
            pltpu.SemaphoreType.DMA((2, nb - 1)),
            pltpu.SemaphoreType.DMA((3,)),
            pltpu.SemaphoreType.DMA((nb - 1,)),
            pltpu.SemaphoreType.DMA((nb - 1,)),
        ],
        compiler_params=pltpu.CompilerParams(collective_id=0, has_side_effects=True),
        cost_estimate=pl.CostEstimate(flops=10**11, bytes_accessed=10**8, transcendentals=0),
        name="exchange",
    )(warm, wet, fading)


def ends_kernel(weights, x, ends):
    for f in range(2):
        for b in range(x.shape[1]):
            rows = jnp.dot(weights[f, b], x[f, b], preferred_element_type=jnp.float32)
            ends[f, b : b + 1, :] = jnp.sum(rows, axis=0, keepdims=True)


def block_ends(weights, x, sub):
    _, nb, hours, width = x.shape
    return pl.pallas_call(
        ends_kernel,
        grid=(width // sub,),
        out_shape=jax.ShapeDtypeStruct((2, nb, width), jnp.float32),
        in_specs=[
            pl.BlockSpec(weights.shape, lambda i: (0, 0, 0, 0)),
            pl.BlockSpec((2, nb, hours, sub), lambda i: (0, 0, 0, i)),
        ],
        out_specs=pl.BlockSpec((2, nb, sub), lambda i: (0, 0, i)),
        compiler_params=pltpu.CompilerParams(vmem_limit_bytes=VMEM_LIMIT),
        name="block_ends",
    )(weights, x)


def anomaly_kernel(nt, nz, gains, within, fade, ends, own, start, x, operator, anomaly, proj, total):
    nb = nt * 2
    z_mine = lax.axis_index("zz")

    @pl.when(pl.program_id(0) == 0)
    def _():
        total[...] = jnp.zeros_like(total)

    for f in range(2):
        level = start[0, f : f + 1, :]
        entering = [level] * nb
        for t in range(nt):
            for z in range(nz):
                step = t * nz + z
                entering[t * 2] = jnp.where(z_mine == z, level, entering[t * 2])
                level = (
                    gains[f, step * 2] * gains[f, step * 2 + 1] * level + ends[z, f, t : t + 1, :]
                )
            first = gains[f, (t * nz + z_mine) * 2]
            entering[t * 2 + 1] = first * entering[t * 2] + own[f, t * 2 : t * 2 + 1, :]
        for b in range(nb):
            values = x[f, b]
            twice = jnp.concatenate([values, values], axis=0)
            inside = jnp.dot(within[f, b], twice, preferred_element_type=jnp.float32)
            previous = inside + fade[f, b] * entering[b]
            departure = (values.astype(jnp.float32) - previous).astype(jnp.bfloat16)
            anomaly[f, b] = departure
            total[b, f] += jnp.dot(departure, operator[0, f], preferred_element_type=jnp.float32)

    @pl.when(pl.program_id(0) == pl.num_programs(0) - 1)
    def _():
        proj[...] = total[...].astype(proj.dtype)


def anomalies(gains, within, fade, ends, own, start, x, operator, nt, nz, sub):
    _, nb, hours, width = x.shape
    rank = operator.shape[-1]
    return pl.pallas_call(
        functools.partial(anomaly_kernel, nt, nz),
        grid=(nz,),
        out_shape=(
            jax.ShapeDtypeStruct(x.shape, jnp.bfloat16),
            jax.ShapeDtypeStruct((nb, 2, hours, rank), jnp.bfloat16),
        ),
        in_specs=[
            pl.BlockSpec(memory_space=pltpu.SMEM),
            pl.BlockSpec(within.shape, lambda i: (0, 0, 0, 0)),
            pl.BlockSpec(fade.shape, lambda i: (0, 0, 0, 0)),
            pl.BlockSpec((nz, 2, nt, sub), lambda i: (0, 0, 0, i)),
            pl.BlockSpec((2, nb, sub), lambda i: (0, 0, i)),
            pl.BlockSpec((1, 2, sub), lambda i: (i, 0, 0)),
            pl.BlockSpec((2, nb, hours, sub), lambda i: (0, 0, 0, i)),
            pl.BlockSpec((1, 2, sub, rank), lambda i: (i, 0, 0, 0)),
        ],
        out_specs=(
            pl.BlockSpec((2, nb, hours, sub), lambda i: (0, 0, 0, i)),
            pl.BlockSpec((nb, 2, hours, rank), lambda i: (0, 0, 0, 0)),
        ),
        scratch_shapes=[pltpu.VMEM((nb, 2, hours, rank), jnp.float32)],
        compiler_params=pltpu.CompilerParams(vmem_limit_bytes=VMEM_LIMIT),
        name="anomalies",
    )(gains, within, fade, ends, own, start, x, operator)


def over_hours(left, right):
    return lax.dot_general(
        left, right, (((0,), (0,)), ((), ())), preferred_element_type=jnp.float32
    )


def sketch_kernel(
    nt, nz, sub, proj, anomaly, sketch, middle,
    held, parts, lines, cross, planes, rows,
    load_sem, part_send, part_recv, line_send, line_recv,
    plane_send, plane_recv, row_send, row_recv,
):
    nb = nt * 2
    t, z, c = lax.axis_index("tm"), lax.axis_index("zz"), lax.axis_index("cc")
    mine = t * 2 + c
    hours, rank = proj.shape[2:]
    share = rank // nb
    masks = range(1, nb)
    load = pltpu.make_async_copy(anomaly, held, load_sem)
    load.start()

    def z_peer(step):
        return (t, lax.rem(z + step, nz), c)

    barrier = pltpu.get_barrier_semaphore()
    for mask in masks:
        pl.semaphore_signal(barrier, inc=1, device_id=group_peer(mask, nb)[1], device_id_type=MESH)
    for step in range(1, nz):
        pl.semaphore_signal(barrier, inc=1, device_id=z_peer(step), device_id_type=MESH)
    pl.semaphore_wait(barrier, nb - 1 + nz - 1)

    def to_group(mask, src, dst, send, recv):
        return pltpu.make_async_remote_copy(
            src_ref=src,
            dst_ref=dst,
            send_sem=send.at[mask - 1],
            recv_sem=recv.at[mask - 1],
            device_id=group_peer(mask, nb)[1],
            device_id_type=MESH,
        )

    copies = [
        to_group(m, proj.at[group_peer(m, nb)[0]], parts.at[m - 1], part_send, part_recv)
        for m in masks
    ]
    for copy in copies:
        copy.start()
    total = proj[mine].astype(jnp.float32)
    for m, copy in zip(masks, copies):
        copy.wait_recv()
        total = total + parts[m - 1].astype(jnp.float32)
    lines[mine] = total.astype(jnp.bfloat16)
    for copy in copies:
        copy.wait_send()
    copies = [
        to_group(m, lines.at[mine], lines.at[mine], line_send, line_recv) for m in masks
    ]
    for copy in copies:
        copy.start()
    load.wait()
    for copy in copies:
        copy.wait()

    left = lines[:, 0].reshape(nb * hours, rank)
    right = lines[:, 1].reshape(nb * hours, rank)
    cross[...] = over_hours(left, right).reshape(nb, share, rank)
    copies = [
        pltpu.make_async_remote_copy(
            src_ref=cross.at[mine],
            dst_ref=planes.at[step - 1],
            send_sem=plane_send.at[step - 1],
            recv_sem=plane_recv.at[step - 1],
            device_id=z_peer(step),
            device_id_type=MESH,
        )
        for step in range(1, nz)
    ]
    for copy in copies:
        copy.start()

    def columns(i, f):
        cut = pl.ds(pl.multiple_of(i * sub, 128), sub)
        values = held[f, :, :, cut].reshape(nb * hours, sub)
        weights = lines[:, 1 - f].reshape(nb * hours, rank)
        sketch[f, :, cut] = over_hours(weights, values).astype(jnp.bfloat16)

    @pl.loop(0, nz)
    def _(i):
        columns(i, 0)

    for copy in copies:
        copy.wait()
    ordered = [cross[mine]] + [planes[step - 1] for step in range(1, nz)]
    summed = jnp.zeros_like(ordered[0])
    for plane in range(nz):
        for step in range(nz):
            summed = summed + jnp.where(lax.rem(z - step + nz, nz) == plane, ordered[step], 0.0)
    rows[mine] = summed
    copies = [to_group(m, rows.at[mine], rows.at[mine], row_send, row_recv) for m in masks]
    for copy in copies:
        copy.start()

    @pl.loop(0, nz)
    def _(i):
        columns(i, 1)

    for copy in copies:
        copy.wait()
    middle[...] = rows[...].reshape(rank, rank)


def sketches_of(proj, anomaly, nt, nz, sub):
    nb, _, hours, rank = proj.shape
    dma = pltpu.SemaphoreType.DMA
    return pl.pallas_call(
        functools.partial(sketch_kernel, nt, nz, sub),
        out_shape=(
            jax.ShapeDtypeStruct((2, rank, nz * sub), jnp.bfloat16),
            jax.ShapeDtypeStruct((rank, rank), jnp.float32),
        ),
        in_specs=[pl.BlockSpec(memory_space=pltpu.VMEM), pl.BlockSpec(memory_space=pl.ANY)],
        out_specs=(pl.BlockSpec(memory_space=pltpu.VMEM),) * 2,
        scratch_shapes=[
            pltpu.VMEM(anomaly.shape, jnp.bfloat16),
            pltpu.VMEM((nb - 1, 2, hours, rank), jnp.bfloat16),
            pltpu.VMEM((nb, 2, hours, rank), jnp.bfloat16),
            pltpu.VMEM((nb, rank // nb, rank), jnp.float32),
            pltpu.VMEM((nz - 1, rank // nb, rank), jnp.float32),
            pltpu.VMEM((nb, rank // nb, rank), jnp.float32),
            dma,
            dma((nb - 1,)),
            dma((nb - 1,)),
            dma((nb - 1,)),
            dma((nb - 1,)),
            dma((nz - 1,)),
            dma((nz - 1,)),
            dma((nb - 1,)),
            dma((nb - 1,)),
        ],
        compiler_params=pltpu.CompilerParams(
            collective_id=1, has_side_effects=True, vmem_limit_bytes=VMEM_LIMIT
        ),
        name="sketches",
    )(proj, anomaly)


def split(weights, count):
    parts = []
    for _ in range(count):
        part = lax.reduce_precision(weights, 8, 7)
        parts.append(part.astype(jnp.bfloat16))
        weights = weights - part
    return parts


def per_device(warm, wet, fading, starting, warmth_operator, wetness_operator):
    nt, nz = lax.axis_size("tm"), lax.axis_size("zz")
    t_mine, z_mine = lax.axis_index("tm"), lax.axis_index("zz")
    nb = nt * 2
    hours = warm.shape[0]
    sub = warm.shape[1] // (nb * nz)
    rank = warmth_operator.shape[1]

    tile = jnp.stack([warmth_operator, wetness_operator])
    average = jnp.stack(split(lax.dynamic_slice_in_dim(starting, t_mine * sub, sub, axis=1), 3), 1)
    average = average.reshape(2, -1, rank)
    extra = average.shape[1]
    average = jnp.pad(average, ((0, 0), (0, -extra % 16), (0, 0)))
    tile = lax.dynamic_slice_in_dim(tile, t_mine * sub, sub, axis=1)
    tiles = lax.all_gather(jnp.concatenate([tile, average], axis=1), "zz")
    terms = tiles[:, :, sub : sub + extra].reshape(nz, 2, 3, sub).astype(jnp.float32)
    start = terms[:, :, 0] + terms[:, :, 1] + terms[:, :, 2]

    x, decays = exchange(warm, wet, fading, nt, nz, sub)
    fading = jnp.concatenate([decays[2 * t] for t in range(nt)], axis=1)

    every = fading.reshape(2, nt, nz, 2, hours)
    gains = jnp.exp(jnp.sum(jnp.log(every), axis=-1)).reshape(2, nt * nz * 2)
    decay = lax.dynamic_index_in_dim(every, z_mine, 2, keepdims=False).reshape(2, nb, hours)
    log_decay = jnp.log(decay)
    row = lax.broadcasted_iota(jnp.int32, (hours, hours), 0)
    col = lax.broadcasted_iota(jnp.int32, (hours, hours), 1)
    inclusive = jnp.sum(jnp.where(row >= col, log_decay[:, :, None, :], 0.0), axis=-1)
    exclusive = inclusive - log_decay
    spread = exclusive[..., :, None] - inclusive[..., None, :]
    within = (
        jnp.where(row > col, jnp.exp(jnp.minimum(spread, 0.0)), 0.0)
        * (1.0 - decay)[..., None, :]
    )
    within = jnp.concatenate(split(within, 2), axis=-1)
    to_end = jnp.exp(inclusive[..., -1:] - inclusive) * (1.0 - decay)
    to_end = jnp.stack(split(to_end, 3), axis=2)
    to_end = jnp.pad(to_end, ((0, 0), (0, 0), (0, 13), (0, 0)))
    fade = jnp.exp(exclusive)[..., None]

    own = block_ends(to_end, x, sub)
    pairs = own.reshape(2, nt, 2, nz * sub)
    second = jnp.exp(inclusive[..., -1]).reshape(2, nt, 2)[:, :, 1, None]
    ends = lax.all_gather(second * pairs[:, :, 0] + pairs[:, :, 1], "zz")
    anomaly, proj = anomalies(gains, within, fade, ends, own, start, x, tiles, nt, nz, sub)
    sketches, middle = sketches_of(proj, anomaly, nt, nz, sub)
    scale = (nb * nz * hours) ** (-0.5)
    sums = lax.psum_scatter(sketches, "zz", scatter_dimension=2, tiled=True)
    sums = lax.all_to_all(sums, "tm", split_axis=1, concat_axis=2, tiled=True)
    sums = sums.astype(jnp.float32) * scale
    return sums[0], sums[1], middle * scale


def solution(mesh):
    nt, ng = mesh.devices.shape
    mesh = Mesh(mesh.devices.reshape(nt, ng // 2, 2), ("tm", "zz", "cc"))
    grid = ("zz", "cc")
    return jax.shard_map(
        per_device,
        mesh=mesh,
        in_specs=(
            P(("tm", "zz", "cc"), None),
            P(("tm", "zz", "cc"), None),
            P(None, "tm"),
            P(None, grid),
            P(grid, None),
            P(grid, None),
        ),
        out_specs=(P("tm", grid), P("tm", grid), P()),
        check_vma=False,
    )
```
